32 devices in a mesh: leaf: 4 (over z), expert: 4 (over y, x), tensor: 2 (over core).
Axes of the slice: x: 2, y: 2, z: 4, core: 2. Of those that a mesh axis runs over, the one named last changes fastest.
Arguments:
- drafts: bfloat16 [1024, 6144], P('leaf', ('expert', 'tensor')), may hold values from -6 to 6
- children: bfloat16 [2048, 6144], P('leaf', ('expert', 'tensor')), may hold values from -6 to 6
- child_order: int32 [8], replicated, may hold values from 0 to 7, each once
- spans: int32 [2048], P('leaf'), may hold values from 0 to 15
- span_bias: float32 [48, 16], P(('expert', 'tensor')), may hold values from -4 to 4
- out_weight: bfloat16 [6144, 6144], P(('expert', 'tensor')), may hold values from -0.078125 to 0.078125
- norm_gain: float32 [6144], replicated, may hold values from 0.1 to 1.9
- router: bfloat16 [6144, 4], replicated, may hold values from -0.078125 to 0.078125
- routes: int32 [1024, 2], P(('leaf', 'expert')), may hold values from 0 to 3, all different within a row; in each aligned block of 64 rows (0 to 63, 64 to 127, ...) at most 64 rows name the same one
- w_gate: bfloat16 [4, 6144, 8192], P('expert', None, ('leaf', 'tensor')), may hold values from -0.078125 to 0.078125
- w_up: bfloat16 [4, 6144, 8192], P('expert', None, ('leaf', 'tensor')), may hold values from -0.078125 to 0.078125
- w_down: bfloat16 [4, 8192, 6144], P('expert', ('leaf', 'tensor')), may hold values from -0.0625 to 0.0625
Outputs:
- merged_out: float32 [1024, 6144], P(('leaf', 'expert'))
The draws below stay inside these ranges and needn't reach their ends.
Inputs may be any that keep to these rules, and one draw needn't show every extreme that they name: `routes`: each row names two different experts; within the rows of one index pair of leaf and expert (64 aligned rows) no expert is named more than 64 times, and exactly 64 times in some of them. `child_order`: A permutation: every parent has exactly two children.
All inputs are finite; a program needn't handle non-finite values.
Results may differ from the reference program's by a relative error of at most 0.013.
Values may be sent and summed in bfloat16 or wider, within the bound.
A program may use at most 128 MiB of HBM per device.

```python
import math
import jax
import jax.numpy as jnp
import numpy as np
from jax import lax

D = 6144
HEADS = 48
HD = 128
FFW = 8192
R = 256
SPANS = 16
PARENTS = 4
CHILDREN = 8
TOKENS = 1024
TOK_DEV = 64
EXPERTS = 4
CAP = 64
N_LEAF = 4
N_TENSOR = 2


def planted_pattern(key):
    folded = jax.random.fold_in(key, 9173)
    pieces = jax.random.split(folded, 4)
    head_pick = jax.random.randint(pieces[0], (), 0, HEADS)
    sign_table = jnp.where(jax.random.bernoulli(pieces[1], 0.5, (HD,)), 1.0, -1.0).astype(jnp.float32)
    query_start = jax.random.randint(pieces[2], (), 0, R)
    key_start = jax.random.randint(pieces[3], (), 0, R)
    return (head_pick, sign_table, query_start, key_start)


def base_values(key, count, salt):
    folded = jax.random.fold_in(key, salt)
    return jnp.clip(jax.random.normal(folded, (count, D), jnp.float32), -6.0, 6.0)


def column_layout(head_pick, sign_table):
    column = jnp.arange(D, dtype=jnp.int32)
    in_head = column // HD == head_pick
    feature = column % HD
    aligned = feature < 3 * HD // 4
    pattern = jnp.take(sign_table, feature)
    return (in_head, aligned, pattern)


def draw_drafts(key, part):
    head_pick, sign_table, query_start, key_start = planted_pattern(key)
    values = base_values(key, TOKENS, 4211)
    in_head, aligned, pattern = column_layout(head_pick, sign_table)
    position = jnp.arange(TOKENS, dtype=jnp.int32) % R
    heights = (3.0, 4.5, 5.5)
    strength = jnp.zeros((TOKENS,), jnp.float32)
    chosen_rows = jnp.zeros((TOKENS,), bool)
    for turn_index, height in enumerate(heights):
        hit = position == (query_start + turn_index * (R // 3)) % R
        strength = jnp.where(hit, height, strength)
        chosen_rows = chosen_rows | hit
    planted = jnp.where(aligned[None, :], strength[:, None] * pattern[None, :], 0.0)
    result = jnp.where(chosen_rows[:, None] & in_head[None, :], planted, values)
    return result.astype(jnp.bfloat16)


def draw_children(key, part):
    head_pick, sign_table, query_start, key_start = planted_pattern(key)
    total_rows = CHILDREN * R
    values = base_values(key, total_rows, 7723)
    in_head, aligned, pattern = column_layout(head_pick, sign_table)
    position = jnp.arange(total_rows, dtype=jnp.int32) % R
    strength = jnp.zeros((total_rows,), jnp.float32)
    chosen_rows = jnp.zeros((total_rows,), bool)
    for turn_index in range(4):
        hit = position == (key_start + turn_index * (R // 4)) % R
        strength = jnp.where(hit, 6.0 - 0.0625 * turn_index, strength)
        chosen_rows = chosen_rows | hit
    planted = strength[:, None] * pattern[None, :]
    replace = chosen_rows[:, None] & in_head[None, :] & aligned[None, :]
    result = jnp.where(replace, planted, values)
    return result.astype(jnp.bfloat16)


def touch_ends(array, stream_key, smallest, largest):
    longest = array.shape.index(max(array.shape))
    spots = []
    for shift in (0, 1):
        where = [jax.random.randint(jax.random.fold_in(stream_key, axis), (), 0, length) for axis, length in enumerate(array.shape)]
        where[longest] = (where[longest] + shift) % array.shape[longest]
        spots.append(tuple(where))
    return array.at[spots[0]].set(smallest).at[spots[1]].set(largest)


def block_scale(key, shape, cuts, smallest, top_value):
    factor_of, own = 1.0, jax.random.fold_in(key, 6)
    for axis_at, shards_of in cuts:
        steps = jnp.exp(jax.random.uniform(jax.random.fold_in(own, axis_at), (shards_of,), jnp.float32, smallest / len(cuts), top_value / len(cuts)))
        factor_of = factor_of * jnp.repeat(steps, shape[axis_at] // shards_of).reshape([-1 if axis == axis_at else 1 for axis in range(len(shape))])
    return factor_of


def routed_block(key, own, number, rows, count, top, reach, skew):
    sequence = jax.random.permutation(key, count)
    heavy_load, usual = shares(count, rows * top, reach, skew, True), shares(count, rows * top, reach, skew, False)
    places = jnp.arange(count)

    def named(lengths, offset_by):
        used = int((lengths > 0).sum())
        fixed = max(1, used // 4)
        shifted = fixed + (places - fixed + offset_by * (used - fixed)) % max(1, count - fixed)
        return jnp.zeros((count,), jnp.int32).at[sequence[jnp.where(places < fixed, places, shifted)]].set(jnp.asarray(lengths, jnp.int32))

    lengths = jnp.where(number % 4 == 0, named(heavy_load, number // 4), named(usual, number - number // 4 - 1))
    mixed = jax.random.permutation(jax.random.fold_in(own, 3), count)
    source_of, sink = mixed[0:count // 2 * 2:2], mixed[1:count // 2 * 2:2]
    room = jnp.minimum(lengths[source_of] - 1, reach - lengths[sink]) // 2
    room = jnp.where((source_of == sequence[0]) | (sink == sequence[0]) | (lengths[sink] == 0), 0, jnp.maximum(room, 0))
    shifted = jax.random.randint(jax.random.fold_in(own, 4), (count // 2,), 0, 1 << 20) % (room + 1)
    lengths = lengths.at[source_of].add(-shifted).at[sink].add(shifted)
    labels = jnp.searchsorted(jnp.cumsum(lengths), jnp.arange(rows * top), side="right").astype(jnp.int32)
    grid = labels.reshape(top, rows).T
    grid = grid[jax.random.permutation(jax.random.fold_in(own, 1), rows)]
    offset_by = jax.random.randint(jax.random.fold_in(own, 2), (rows, 1), 0, top)
    return jnp.take_along_axis(grid, (jnp.arange(top)[None, :] + offset_by) % top, axis=1)


def shares(count, total, bound, slope, full):
    portions = [(1 << 20) // math.isqrt(standing ** slope) + 1 for standing in range(1, count + 1)]
    largest = bound if full else min(bound, max(-(-total // count), total * portions[0] // sum(portions)))
    least = 1 if total - largest >= count - 1 else 0
    holding, spare = [largest] + [least] * (count - 1), total - largest - least * (count - 1)
    while spare > 0:
        free = [i for i in range(1, count) if holding[i] < largest] or [i for i in range(1, count) if holding[i] < bound]
        whole, budget = sum([portions[i] for i in free]), spare
        for i in free:
            addition = min(bound - holding[i], max(1, budget * portions[i] // whole), spare)
            holding[i] = holding[i] + addition
            spare = spare - addition
    return np.array(holding)


def bell_draw(rng, extent, deviation, limit, cuts=(), kind=jnp.bfloat16):
    values = jax.random.normal(rng, extent, jnp.float32) * deviation
    if len(cuts) > 0:
        values = block_scale(rng, extent, cuts, -0.22, 0.18) * values
    return jnp.clip(values, min=-limit, max=limit).astype(kind)


def setup_inputs(seed: int = 0) -> dict:
    seeds = jax.random.split(jax.random.key(seed), 13)
    drafts = draw_drafts(jax.random.fold_in(seeds[12], 71), 0)
    children = draw_children(jax.random.fold_in(seeds[12], 71), 0)
    child_order = jax.random.permutation(seeds[2], CHILDREN).astype(jnp.int32)
    spans = touch_ends(jax.random.randint(seeds[3], (CHILDREN * R,), 0, SPANS), jax.random.fold_in(seeds[3], 1), 0, SPANS - 1).astype(jnp.int32)
    span_bias = bell_draw(seeds[4], (HEADS, SPANS), 1.0, 4.0, ((0, 8),), jnp.float32)
    out_weight = bell_draw(seeds[5], (D, D), D ** -0.5, 0.078125, ((0, 8),))
    norm_gain = jnp.clip(1.0 + 0.18 * jax.random.normal(seeds[6], (D,), jnp.float32), 0.1, 1.9)
    router = bell_draw(seeds[7], (D, EXPERTS), D ** -0.5, 0.078125)
    routes_keys = jax.random.split(jax.random.fold_in(seeds[8], 1), TOKENS // TOK_DEV)
    routes_turns = jax.random.permutation(jax.random.fold_in(seeds[8], 3), TOKENS // TOK_DEV)
    routes = jax.vmap(lambda own, number: routed_block(jax.random.fold_in(seeds[8], 2), own, number, TOK_DEV, EXPERTS, 2, CAP, 2))(routes_keys, routes_turns).reshape((TOKENS, 2))
    w_gate = bell_draw(seeds[9], (EXPERTS, D, FFW), D ** -0.5, 0.078125, ((0, 4), (2, 8)))
    w_up = bell_draw(seeds[10], (EXPERTS, D, FFW), D ** -0.5, 0.078125, ((0, 4), (2, 8)))
    w_down = bell_draw(seeds[11], (EXPERTS, FFW, D), FFW ** -0.5, 0.0625, ((0, 4), (1, 8)))
    return dict(drafts=drafts, children=children, child_order=child_order, spans=spans, span_bias=span_bias, out_weight=out_weight, norm_gain=norm_gain, router=router, routes=routes, w_gate=w_gate, w_up=w_up, w_down=w_down)


def reference(drafts, children, child_order, spans, span_bias, out_weight, norm_gain, router, routes, w_gate, w_up, w_down):
    width = drafts.shape[1]
    head_size = width // HEADS
    scale = 1.0 / math.sqrt(head_size)
    count = child_order.shape[0]
    inverse = jnp.zeros((count,), jnp.int32).at[child_order].set(jnp.arange(count, dtype=jnp.int32))

    def merge_parent(parent):
        queries = lax.dynamic_slice_in_dim(drafts, (parent * R).astype(jnp.int32), R, 0)
        first = inverse[2 * parent]
        second = inverse[2 * parent + 1]
        keys = jnp.concatenate([lax.dynamic_slice_in_dim(children, (first * R).astype(jnp.int32), R, 0), lax.dynamic_slice_in_dim(children, (second * R).astype(jnp.int32), R, 0)], axis=0)
        key_spans = jnp.concatenate([lax.dynamic_slice_in_dim(spans, (first * R).astype(jnp.int32), R, 0), lax.dynamic_slice_in_dim(spans, (second * R).astype(jnp.int32), R, 0)], axis=0)
        query_f = queries.astype(jnp.float32).reshape(R, HEADS, head_size)
        key_f = keys.astype(jnp.float32).reshape(2 * R, HEADS, head_size)
        scores = jnp.einsum('qhd,khd->hqk', query_f, key_f, precision=lax.Precision.HIGHEST) * scale
        scores = scores + span_bias[:, key_spans][:, None, :]
        probs = jax.nn.softmax(scores, axis=-1)
        attended = jnp.einsum('hqk,khd->qhd', probs, key_f, precision=lax.Precision.HIGHEST)
        return attended.reshape(R, width).astype(jnp.bfloat16)
    attended = lax.map(merge_parent, jnp.arange(PARENTS, dtype=jnp.int32)).reshape(PARENTS * R, width)
    merged = drafts.astype(jnp.float32) + jnp.dot(attended, out_weight, preferred_element_type=jnp.float32)
    mean_square = lax.optimization_barrier(jnp.mean(merged * merged, axis=-1, keepdims=True))
    normed = (merged * lax.rsqrt(mean_square + 1e-05) * norm_gain).astype(jnp.bfloat16)
    logits = jnp.dot(normed, router, preferred_element_type=jnp.float32)
    experts = router.shape[1]
    expert_hot = routes[:, :, None] == jnp.arange(experts, dtype=jnp.int32)[None, None, :]
    chosen = lax.optimization_barrier(jnp.sum(jnp.where(expert_hot, logits[:, None, :], 0.0), axis=-1))
    gates = jax.nn.softmax(chosen, axis=-1)
    blocks = routes.shape[0] // TOK_DEV
    pairs = routes.reshape(blocks, 2 * TOK_DEV)
    pair_hot = (pairs[:, :, None] == jnp.arange(experts, dtype=jnp.int32)[None, None, :]).astype(jnp.int32)
    earlier = jnp.cumsum(pair_hot, axis=1) - pair_hot
    slot_index = lax.optimization_barrier(jnp.sum(earlier * pair_hot, axis=-1))
    block_ids = jnp.broadcast_to(jnp.arange(blocks, dtype=jnp.int32)[:, None], pairs.shape)
    rows = jnp.repeat(normed.reshape(blocks, TOK_DEV, width), 2, axis=1)
    buffers = jnp.zeros((experts, blocks, CAP, width), jnp.bfloat16)
    buffers = buffers.at[pairs, block_ids, slot_index].set(rows)
    buffers = buffers.reshape(experts, blocks * CAP, width)
    pieces = N_LEAF * N_TENSOR
    piece_width = w_gate.shape[2] // pieces

    def run_expert(operands):
        inputs, gate_w, up_w, down_w = operands
        gate_blocks = gate_w.reshape(width, pieces, piece_width).transpose(1, 0, 2)
        up_blocks = up_w.reshape(width, pieces, piece_width).transpose(1, 0, 2)
        down_blocks = down_w.reshape(pieces, piece_width, width)

        def add_piece(total, weights):
            gate_b, up_b, down_b = weights
            gate_v = jnp.dot(inputs, gate_b, preferred_element_type=jnp.float32)
            up_v = jnp.dot(inputs, up_b, preferred_element_type=jnp.float32)
            hidden = (jax.nn.silu(gate_v) * up_v).astype(jnp.bfloat16)
            part = jnp.dot(hidden, down_b, preferred_element_type=jnp.float32).astype(jnp.bfloat16)
            return (total + part.astype(jnp.float32), None)
        total, unused = lax.scan(add_piece, jnp.zeros((blocks * CAP, width), jnp.float32), (gate_blocks, up_blocks, down_blocks))
        return total.astype(jnp.bfloat16)
    outputs = lax.map(run_expert, (buffers, w_gate, w_up, w_down)).reshape(experts, blocks, CAP, width)
    picked = outputs[pairs, block_ids, slot_index].astype(jnp.float32).reshape(blocks * TOK_DEV, 2, width)
    mixed = gates[:, 0:1] * picked[:, 0] + gates[:, 1:2] * picked[:, 1]
    return (merged + mixed).astype(jnp.float32)
```

```python
import math

import jax
import jax.numpy as jnp
from jax import lax
from jax.experimental import pallas as pl
from jax.experimental.pallas import tpu as pltpu
from jax.sharding import PartitionSpec as P

R = 256


def attend_kernel(groups, halves, span_count, ids, bias_ref, q_ref, ka_ref, kb_ref, sa_ref, sb_ref, o_ref):
    head = pl.program_id(0)
    scale = 1.0 / math.sqrt(q_ref.shape[1])
    queries = q_ref[...]
    contract = (((1,), (1,)), ((), ()))

    def score(k_ref, s_ref):
        spans = s_ref[0]
        bias = jnp.zeros(spans.shape, jnp.float32)
        for span in range(span_count):
            bias = jnp.where(spans == span, bias_ref[head, span], bias)
        dots = lax.dot_general(queries, k_ref[...], contract, preferred_element_type=jnp.float32)
        return dots * scale + bias

    score_a = score(ka_ref, sa_ref)
    score_b = score(kb_ref, sb_ref)
    top = jnp.maximum(
        jnp.max(score_a, axis=-1, keepdims=True), jnp.max(score_b, axis=-1, keepdims=True)
    )
    weight_a = jnp.exp(score_a - top)
    weight_b = jnp.exp(score_b - top)
    total = jnp.sum(weight_a, axis=-1, keepdims=True) + jnp.sum(weight_b, axis=-1, keepdims=True)
    values = jnp.dot(
        weight_a.astype(jnp.bfloat16), ka_ref[...], preferred_element_type=jnp.float32
    ) + jnp.dot(weight_b.astype(jnp.bfloat16), kb_ref[...], preferred_element_type=jnp.float32)
    attended = (values / total).astype(jnp.bfloat16)
    rows = attended.shape[0] // (groups * halves)
    for group in range(groups):
        for half in range(halves):
            source = (group * halves + half) * rows
            target = (half * groups + group) * rows
            o_ref[target : target + rows, :] = attended[source : source + rows, :]


def attend(drafts, keys, spans, ids, span_bias, groups, halves):
    rows, width = drafts.shape
    heads = span_bias.shape[0]
    size = width // heads
    return pl.pallas_call(
        lambda *refs: attend_kernel(groups, halves, span_bias.shape[1], *refs),
        out_shape=jax.ShapeDtypeStruct((rows, width), jnp.bfloat16),
        grid_spec=pltpu.PrefetchScalarGridSpec(
            num_scalar_prefetch=1,
            grid=(heads,),
            in_specs=[
                pl.BlockSpec(memory_space=pltpu.SMEM),
                pl.BlockSpec((rows, size), lambda h, ids: (0, h)),
                pl.BlockSpec((R, size), lambda h, ids: (ids[0], h)),
                pl.BlockSpec((R, size), lambda h, ids: (ids[1], h)),
                pl.BlockSpec((1, 1, R), lambda h, ids: (ids[0], 0, 0)),
                pl.BlockSpec((1, 1, R), lambda h, ids: (ids[1], 0, 0)),
            ],
            out_specs=pl.BlockSpec((rows, size), lambda h, ids: (0, h)),
        ),
        cost_estimate=pl.CostEstimate(
            flops=8 * rows * R * width, bytes_accessed=8 * rows * width, transcendentals=2 * rows * R * heads
        ),
    )(ids, span_bias, drafts, keys, keys, spans, spans)


def per_device(
    drafts,
    children,
    child_order,
    spans,
    span_bias,
    out_weight,
    norm_gain,
    router,
    routes,
    w_gate,
    w_up,
    w_down,
):
    leaves = lax.axis_size("leaf")
    groups = lax.axis_size("expert")
    halves = lax.axis_size("tensor")
    width = out_weight.shape[1]
    rows = drafts.shape[0] // (groups * halves)
    swap = [(index, index ^ 1) for index in range(halves)]
    parent = lax.axis_index("leaf")
    expert = lax.axis_index("expert")
    half = lax.axis_index("tensor")

    keys = lax.all_gather(children, "leaf", axis=0, tiled=True)
    key_spans = lax.all_gather(spans, "leaf", axis=0, tiled=True).reshape(-1, 1, R)
    all_routes = lax.all_gather(routes, ("leaf", "expert"), axis=0, tiled=True)
    draft_rows = lax.all_to_all(
        drafts, ("expert", "tensor"), split_axis=0, concat_axis=1, tiled=True
    )
    places = jnp.arange(child_order.shape[0], dtype=jnp.int32)
    ids = jnp.stack(
        [
            jnp.sum(jnp.where(child_order == 2 * parent, places, 0)),
            jnp.sum(jnp.where(child_order == 2 * parent + 1, places, 0)),
        ]
    ).astype(jnp.int32)
    attended = attend(drafts, keys, key_spans, ids, span_bias, groups, halves)
    term = jnp.dot(attended, out_weight, preferred_element_type=jnp.float32).astype(jnp.bfloat16)
    term = lax.psum_scatter(term, "tensor", scatter_dimension=0, tiled=True)
    term = lax.psum_scatter(term, "expert", scatter_dimension=0, tiled=True)
    merged = draft_rows.astype(jnp.float32) + term.astype(jnp.float32)
    mean_square = jnp.mean(merged * merged, axis=-1, keepdims=True)
    normed = (merged * lax.rsqrt(mean_square + 1e-05) * norm_gain).astype(jnp.bfloat16)

    own = lax.all_gather(normed, "leaf", axis=0, tiled=True)
    own = lax.all_gather(own, "expert", axis=0, tiled=True)
    other = lax.ppermute(own, "tensor", swap)
    merged_all = lax.all_gather(merged, "tensor", axis=0, tiled=True)

    routes_at = all_routes.reshape(leaves, groups, halves, rows, 2).transpose(2, 1, 0, 3, 4)
    routes_at = routes_at.reshape(halves, -1, 2)

    def gate_of(block, which):
        named = lax.dynamic_index_in_dim(routes_at, which, 0, keepdims=False)
        logits = jnp.dot(block, router, preferred_element_type=jnp.float32)
        hot = named[:, :, None] == jnp.arange(router.shape[1], dtype=jnp.int32)[None, None, :]
        chosen = jnp.sum(jnp.where(hot, logits[:, None, :], 0.0), axis=-1)
        gates = jax.nn.softmax(chosen, axis=-1)
        return jnp.sum(jnp.where(named == expert, gates, 0.0), axis=-1, keepdims=True)

    def hidden_of(block):
        gate_v = jnp.dot(block, w_gate[0], preferred_element_type=jnp.float32)
        up_v = jnp.dot(block, w_up[0], preferred_element_type=jnp.float32)
        return (jax.nn.silu(gate_v) * up_v).astype(jnp.bfloat16)

    own_gate = gate_of(own, half)
    own_hidden = hidden_of(own)
    other_gate = gate_of(other, 1 - half)
    other_hidden = hidden_of(other)
    other_part = (
        jnp.dot(other_hidden, w_down[0], preferred_element_type=jnp.float32) * other_gate
    ).astype(jnp.bfloat16)
    returned = lax.ppermute(other_part, "tensor", swap)
    own_part = jnp.dot(own_hidden, w_down[0], preferred_element_type=jnp.float32) * own_gate
    part = (own_part + returned.astype(jnp.float32)).astype(jnp.bfloat16)
    part = lax.psum_scatter(part, "expert", scatter_dimension=0, tiled=True)
    part = lax.psum_scatter(part, "leaf", scatter_dimension=0, tiled=True)
    mixed = lax.all_gather(part, "tensor", axis=0, tiled=True)
    return merged_all + mixed.astype(jnp.float32)


def solution(mesh):
    in_specs = (
        P("leaf", ("expert", "tensor")),
        P("leaf", ("expert", "tensor")),
        P(),
        P("leaf"),
        P(("expert", "tensor"), None),
        P(("expert", "tensor"), None),
        P(),
        P(),
        P(("leaf", "expert"), None),
        P("expert", None, ("leaf", "tensor")),
        P("expert", None, ("leaf", "tensor")),
        P("expert", ("leaf", "tensor"), None),
    )
    out_specs = P(("leaf", "expert"), None)
    return jax.shard_map(
        per_device, mesh=mesh, in_specs=in_specs, out_specs=out_specs, check_vma=False
    )
```

```python
import math

import jax
import jax.numpy as jnp
from jax import lax
from jax.experimental import pallas as pl
from jax.experimental.pallas import tpu as pltpu
from jax.sharding import PartitionSpec as P

R = 256


def attend_kernel(groups, halves, span_count, ids, bias_ref, q_ref, ka_ref, kb_ref, sa_ref, sb_ref, o_ref):
    head = pl.program_id(0)
    scale = 1.0 / math.sqrt(q_ref.shape[1])
    queries = q_ref[...]
    contract = (((1,), (1,)), ((), ()))

    def score(k_ref, s_ref):
        spans = s_ref[0]
        bias = jnp.zeros(spans.shape, jnp.float32)
        for span in range(span_count):
            bias = jnp.where(spans == span, bias_ref[head, span], bias)
        dots = lax.dot_general(queries, k_ref[...], contract, preferred_element_type=jnp.float32)
        return dots * scale + bias

    score_a = score(ka_ref, sa_ref)
    score_b = score(kb_ref, sb_ref)
    top = jnp.maximum(
        jnp.max(score_a, axis=-1, keepdims=True), jnp.max(score_b, axis=-1, keepdims=True)
    )
    weight_a = jnp.exp(score_a - top)
    weight_b = jnp.exp(score_b - top)
    total = jnp.sum(weight_a, axis=-1, keepdims=True) + jnp.sum(weight_b, axis=-1, keepdims=True)
    values = jnp.dot(
        weight_a.astype(jnp.bfloat16), ka_ref[...], preferred_element_type=jnp.float32
    ) + jnp.dot(weight_b.astype(jnp.bfloat16), kb_ref[...], preferred_element_type=jnp.float32)
    attended = (values / total).astype(jnp.bfloat16)
    rows = attended.shape[0] // (groups * halves)
    for group in range(groups):
        for half in range(halves):
            source = (group * halves + half) * rows
            target = (half * groups + group) * rows
            o_ref[target : target + rows, :] = attended[source : source + rows, :]


def attend(drafts, keys, spans, ids, span_bias, groups, halves):
    rows, width = drafts.shape
    heads = span_bias.shape[0]
    size = width // heads
    return pl.pallas_call(
        lambda *refs: attend_kernel(groups, halves, span_bias.shape[1], *refs),
        out_shape=jax.ShapeDtypeStruct((rows, width), jnp.bfloat16),
        grid_spec=pltpu.PrefetchScalarGridSpec(
            num_scalar_prefetch=1,
            grid=(heads,),
            in_specs=[
                pl.BlockSpec(memory_space=pltpu.SMEM),
                pl.BlockSpec((rows, size), lambda h, ids: (0, h)),
                pl.BlockSpec((R, size), lambda h, ids: (ids[0], h)),
                pl.BlockSpec((R, size), lambda h, ids: (ids[1], h)),
                pl.BlockSpec((1, 1, R), lambda h, ids: (ids[0], 0, 0)),
                pl.BlockSpec((1, 1, R), lambda h, ids: (ids[1], 0, 0)),
            ],
            out_specs=pl.BlockSpec((rows, size), lambda h, ids: (0, h)),
        ),
        cost_estimate=pl.CostEstimate(
            flops=8 * rows * R * width, bytes_accessed=8 * rows * width, transcendentals=2 * rows * R * heads
        ),
    )(ids, span_bias, drafts, keys, keys, spans, spans)

MESH = pl.DeviceIdType.MESH


def position():
    leaf, expert, half = (lax.axis_index(name) for name in ("leaf", "expert", "tensor"))
    across = expert + 1 - 2 * (expert % 2)
    along = (expert + 2) % 4
    return leaf, expert, half, across, along


def greet(partners):
    barrier = pltpu.get_barrier_semaphore()
    for partner in partners:
        pl.semaphore_signal(barrier, inc=1, device_id=partner, device_id_type=MESH)
    pl.semaphore_wait(barrier, len(partners))


def send(source, target, sems, index, device):
    copy = pltpu.make_async_remote_copy(
        src_ref=source,
        dst_ref=target,
        send_sem=sems.at[0, index],
        recv_sem=sems.at[1, index],
        device_id=device,
        device_id_type=MESH,
    )
    copy.start()
    return copy


def gather_kernel(
    leaves, rows, own_ref, merged_ref, all_ref, pair_ref, local, z_sem, x_sem, y_sem, a_sem, b_sem, swap_sem
):
    leaf, expert, half, across, along = position()
    opposite = 3 - expert
    x_dev, y_dev = (leaf, across, half), (leaf, along, half)
    twin = (leaf, expert, 1 - half)
    z_devs = [((leaf + step) % leaves, expert, half) for step in range(1, leaves)]
    greet([x_dev, y_dev, twin] + z_devs)
    part = rows // 2

    def block(group, step, first=0, count=rows):
        start = (group * leaves + (leaf + leaves - step) % leaves) * rows + first
        return all_ref.at[half, pl.ds(pl.multiple_of(start, 16), count), :]

    copies = []
    keep = pltpu.make_async_copy(own_ref, block(expert, 0), local.at[0])
    keep.start()
    keep_pair = pltpu.make_async_copy(merged_ref, pair_ref.at[half], local.at[1])
    keep_pair.start()
    z_copies = [None]
    for step in range(1, leaves):
        z_copies.append(send(own_ref, block(expert, 0), z_sem, step, z_devs[step - 1]))
    x_copies, y_copies, a_copies, b_copies = {}, {}, {}, {}
    x_copies[0] = send(own_ref, block(expert, 0), x_sem, 0, x_dev)
    y_copies[0] = send(own_ref, block(expert, 0), y_sem, 0, y_dev)
    copies.append(send(own_ref, block(expert, 0), swap_sem, 0, twin))
    copies.append(send(merged_ref, pair_ref.at[half], swap_sem, 4 * leaves, twin))
    order = [0] + sorted(range(1, leaves), key=lambda step: min(step, leaves - step))

    def forward(step):
        x_copies[step].wait_recv()
        a_copies[step] = send(
            block(across, step, 0, part), block(across, step, 0, part), a_sem, step, y_dev
        )
        y_copies[step].wait_recv()
        b_copies[step] = send(
            block(along, step, part, part), block(along, step, part, part), b_sem, step, x_dev
        )
        copies.append(send(block(across, step), block(across, step), swap_sem, leaves + step, twin))
        copies.append(send(block(along, step), block(along, step), swap_sem, 2 * leaves + step, twin))

    for turn in range(1, leaves):
        step = order[turn]
        z_copies[step].wait_recv()
        x_copies[step] = send(block(expert, step), block(expert, step), x_sem, step, x_dev)
        y_copies[step] = send(block(expert, step), block(expert, step), y_sem, step, y_dev)
        copies.append(send(block(expert, step), block(expert, step), swap_sem, step, twin))
        forward(order[turn - 1])
    forward(order[-1])
    for step in order:
        a_copies[step].wait_recv()
        b_copies[step].wait_recv()
        copies.append(
            send(block(opposite, step), block(opposite, step), swap_sem, 3 * leaves + step, twin)
        )
    for copy in copies:
        copy.wait()
    for step in order:
        for group in (x_copies, y_copies, a_copies, b_copies):
            group[step].wait_send()
        if step > 0:
            z_copies[step].wait_send()
    keep.wait()
    keep_pair.wait()


def gather_rows(normed, merged, leaves, groups):
    rows, width = normed.shape
    dma = pltpu.SemaphoreType.DMA
    anywhere = pl.BlockSpec(memory_space=pl.ANY)
    return pl.pallas_call(
        lambda *refs: gather_kernel(leaves, rows, *refs),
        out_shape=(
            jax.ShapeDtypeStruct((2, groups * leaves * rows, width), normed.dtype),
            jax.ShapeDtypeStruct((2, rows, width), merged.dtype),
        ),
        in_specs=[anywhere] * 2,
        out_specs=(anywhere, anywhere),
        scratch_shapes=[dma((2,))]
        + [dma((2, leaves))] * 5
        + [dma((2, 4 * leaves + 1))],
        compiler_params=pltpu.CompilerParams(collective_id=1, has_side_effects=True),
    )(normed, merged)


def scatter_kernel(
    leaves, rows, part_ref, out_ref, in_a, in_b, mid_a, mid_b, last_a, last_b, sums, far,
    a_sem, b_sem, ma_sem, mb_sem, z_sem, swap_sem,
):
    leaf, expert, half, across, along = position()
    opposite = 3 - expert
    x_dev, y_dev = (leaf, across, half), (leaf, along, half)
    twin = (leaf, expert, 1 - half)
    z_devs = [((leaf + step) % leaves, expert, half) for step in range(1, leaves)]
    greet([x_dev, y_dev, twin] + z_devs)
    cut = rows // 2

    def block(group, step, first):
        start = (group * leaves + (leaf + step) % leaves) * rows + first
        return part_ref.at[pl.ds(pl.multiple_of(start, 16), cut), :]

    def wide(ref):
        return ref[...].astype(jnp.float32)

    order = list(range(1, leaves)) + [0]
    first, second, third = {}, {}, {}
    for step in order:
        first[step] = (
            send(block(opposite, step, 0), in_a.at[step, 1], a_sem, 2 * step + 1, x_dev),
            send(block(opposite, step, cut), in_b.at[step, 1], b_sem, 2 * step + 1, y_dev),
            send(block(across, step, 0), in_a.at[step, 0], a_sem, 2 * step, x_dev),
            send(block(along, step, cut), in_b.at[step, 0], b_sem, 2 * step, y_dev),
        )

    def middle(step):
        first[step][0].wait_recv()
        mid_a[step] = (wide(block(along, step, 0)) + wide(in_a.at[step, 1])).astype(jnp.bfloat16)
        to_y = send(mid_a.at[step], last_a.at[step], ma_sem, step, y_dev)
        first[step][1].wait_recv()
        mid_b[step] = (wide(block(across, step, cut)) + wide(in_b.at[step, 1])).astype(jnp.bfloat16)
        to_x = send(mid_b.at[step], last_b.at[step], mb_sem, step, x_dev)
        second[step] = (to_y, to_x)

    def finish(step):
        first[step][2].wait_recv()
        first[step][3].wait_recv()
        second[step][0].wait_recv()
        sum_a = wide(block(expert, step, 0)) + wide(in_a.at[step, 0]) + wide(last_a.at[step])
        sums[step, 0:cut, :] = sum_a.astype(jnp.bfloat16)
        second[step][1].wait_recv()
        sum_b = wide(block(expert, step, cut)) + wide(in_b.at[step, 0]) + wide(last_b.at[step])
        sums[step, cut:rows, :] = sum_b.astype(jnp.bfloat16)
        if step > 0:
            third[step] = send(sums.at[step], far.at[step], z_sem, step, z_devs[step - 1])

    for turn, step in enumerate(order):
        middle(step)
        if turn > 0:
            finish(order[turn - 1])
    finish(order[-1])
    total = wide(sums.at[0])
    for step in range(1, leaves):
        third[step].wait_recv()
        total = total + wide(far.at[step])
    out_ref[half] = total.astype(jnp.bfloat16)
    swapped = send(out_ref.at[half], out_ref.at[half], swap_sem, 0, twin)
    for step in order:
        for copy in first[step] + second[step]:
            copy.wait_send()
        if step > 0:
            third[step].wait_send()
    swapped.wait()


def scatter_rows(part, leaves, groups):
    rows, width = part.shape[0] // (leaves * groups), part.shape[1]
    cut = rows // 2
    dma = pltpu.SemaphoreType.DMA
    kind = part.dtype
    inside = pl.BlockSpec(memory_space=pltpu.VMEM)
    return pl.pallas_call(
        lambda *refs: scatter_kernel(leaves, rows, *refs),
        out_shape=jax.ShapeDtypeStruct((2, rows, width), kind),
        in_specs=[inside],
        out_specs=inside,
        scratch_shapes=[pltpu.VMEM((leaves, 2, cut, width), kind)] * 2
        + [pltpu.VMEM((leaves, cut, width), kind)] * 4
        + [pltpu.VMEM((leaves, rows, width), kind)] * 2
        + [dma((2, 2 * leaves))] * 2
        + [dma((2, leaves))] * 3
        + [dma((2, 1))],
        compiler_params=pltpu.CompilerParams(
            collective_id=2, has_side_effects=True, vmem_limit_bytes=40 * 1024 * 1024
        ),
    )(part)


def per_device(
    drafts,
    children,
    child_order,
    spans,
    span_bias,
    out_weight,
    norm_gain,
    router,
    routes,
    w_gate,
    w_up,
    w_down,
):
    leaves = lax.axis_size("leaf")
    groups = lax.axis_size("expert")
    halves = lax.axis_size("tensor")
    width = out_weight.shape[1]
    rows = drafts.shape[0] // (groups * halves)
    swap = [(index, index ^ 1) for index in range(halves)]
    parent = lax.axis_index("leaf")
    expert = lax.axis_index("expert")
    half = lax.axis_index("tensor")

    keys = lax.all_gather(children, "leaf", axis=0, tiled=True)
    key_spans = lax.all_gather(spans, "leaf", axis=0, tiled=True).reshape(-1, 1, R)
    all_routes = lax.all_gather(routes, ("leaf", "expert"), axis=0, tiled=True)
    draft_rows = lax.all_to_all(
        drafts, ("expert", "tensor"), split_axis=0, concat_axis=1, tiled=True
    )
    places = jnp.arange(child_order.shape[0], dtype=jnp.int32)
    ids = jnp.stack(
        [
            jnp.sum(jnp.where(child_order == 2 * parent, places, 0)),
            jnp.sum(jnp.where(child_order == 2 * parent + 1, places, 0)),
        ]
    ).astype(jnp.int32)
    ids, all_routes, draft_rows = lax.optimization_barrier((ids, all_routes, draft_rows))
    attended = attend(drafts, keys, key_spans, ids, span_bias, groups, halves)
    term = jnp.dot(attended, out_weight, preferred_element_type=jnp.float32).astype(jnp.bfloat16)
    term = lax.psum_scatter(term, "tensor", scatter_dimension=0, tiled=True)
    term = lax.psum_scatter(term, "expert", scatter_dimension=0, tiled=True)
    merged = draft_rows.astype(jnp.float32) + term.astype(jnp.float32)
    mean_square = jnp.mean(merged * merged, axis=-1, keepdims=True)
    normed = (merged * lax.rsqrt(mean_square + 1e-05) * norm_gain).astype(jnp.bfloat16)

    in_kernels = groups == 4 and halves == 2
    if in_kernels:
        every, merged_all = gather_rows(normed, merged, leaves, groups)
    else:
        every = lax.all_gather(normed, "leaf", axis=0, tiled=True)
        every = lax.all_gather(every, "expert", axis=0, tiled=True)
        every = lax.all_gather(every, "tensor", axis=0, tiled=True)
        merged_all = lax.all_gather(merged, "tensor", axis=0, tiled=True)
    every = every.reshape(-1, width)
    merged_all = merged_all.reshape(-1, width)

    named = all_routes.reshape(leaves, groups, halves, rows, 2).transpose(2, 1, 0, 3, 4)
    named = named.reshape(-1, 2)
    hot = named[:, :, None] == jnp.arange(router.shape[1], dtype=jnp.int32)[None, None, :]
    logits = jnp.dot(every, router, preferred_element_type=jnp.float32)
    chosen = jnp.sum(jnp.where(hot, logits[:, None, :], 0.0), axis=-1)
    gates = jax.nn.softmax(chosen, axis=-1)
    gate = jnp.sum(jnp.where(named == expert, gates, 0.0), axis=-1)
    gate = gate.reshape(halves, -1, 1)

    gate_v = jnp.dot(every, w_gate[0], preferred_element_type=jnp.float32)
    up_v = jnp.dot(every, w_up[0], preferred_element_type=jnp.float32)
    hidden = (jax.nn.silu(gate_v) * up_v).astype(jnp.bfloat16)
    hidden = hidden.reshape(halves, -1, hidden.shape[1])

    def product(which):
        block = lax.dynamic_index_in_dim(hidden, which, 0, keepdims=False)
        scale = lax.dynamic_index_in_dim(gate, which, 0, keepdims=False)
        return jnp.dot(block, w_down[0], preferred_element_type=jnp.float32) * scale

    returned = lax.ppermute(product(1 - half).astype(jnp.bfloat16), "tensor", swap)
    part = (product(half) + returned.astype(jnp.float32)).astype(jnp.bfloat16)
    if in_kernels:
        mixed = scatter_rows(part, leaves, groups).reshape(-1, width)
    else:
        part = lax.psum_scatter(part, "expert", scatter_dimension=0, tiled=True)
        part = lax.psum_scatter(part, "leaf", scatter_dimension=0, tiled=True)
        mixed = lax.all_gather(part, "tensor", axis=0, tiled=True)
    return merged_all + mixed.astype(jnp.float32)


def solution(mesh):
    in_specs = (
        P("leaf", ("expert", "tensor")),
        P("leaf", ("expert", "tensor")),
        P(),
        P("leaf"),
        P(("expert", "tensor"), None),
        P(("expert", "tensor"), None),
        P(),
        P(),
        P(("leaf", "expert"), None),
        P("expert", None, ("leaf", "tensor")),
        P("expert", None, ("leaf", "tensor")),
        P("expert", ("leaf", "tensor"), None),
    )
    out_specs = P(("leaf", "expert"), None)
    return jax.shard_map(
        per_device, mesh=mesh, in_specs=in_specs, out_specs=out_specs, check_vma=False
    )
```

```python
import math

import jax
import jax.numpy as jnp
from jax import lax
from jax.experimental import pallas as pl
from jax.experimental.pallas import tpu as pltpu
from jax.sharding import PartitionSpec as P

R = 256


def attend_kernel(groups, halves, span_count, ids, bias_ref, q_ref, ka_ref, kb_ref, sa_ref, sb_ref, o_ref):
    head = pl.program_id(0)
    scale = 1.0 / math.sqrt(q_ref.shape[1])
    queries = q_ref[...]
    contract = (((1,), (1,)), ((), ()))

    def score(k_ref, s_ref):
        spans = s_ref[0]
        bias = jnp.zeros(spans.shape, jnp.float32)
        for span in range(span_count):
            bias = jnp.where(spans == span, bias_ref[head, span], bias)
        dots = lax.dot_general(queries, k_ref[...], contract, preferred_element_type=jnp.float32)
        return dots * scale + bias

    score_a = score(ka_ref, sa_ref)
    score_b = score(kb_ref, sb_ref)
    top = jnp.maximum(
        jnp.max(score_a, axis=-1, keepdims=True), jnp.max(score_b, axis=-1, keepdims=True)
    )
    weight_a = jnp.exp(score_a - top)
    weight_b = jnp.exp(score_b - top)
    total = jnp.sum(weight_a, axis=-1, keepdims=True) + jnp.sum(weight_b, axis=-1, keepdims=True)
    values = jnp.dot(
        weight_a.astype(jnp.bfloat16), ka_ref[...], preferred_element_type=jnp.float32
    ) + jnp.dot(weight_b.astype(jnp.bfloat16), kb_ref[...], preferred_element_type=jnp.float32)
    attended = (values / total).astype(jnp.bfloat16)
    rows = attended.shape[0] // (groups * halves)
    for group in range(groups):
        for half in range(halves):
            source = (group * halves + half) * rows
            target = (half * groups + group) * rows
            o_ref[target : target + rows, :] = attended[source : source + rows, :]


def attend(drafts, keys, spans, ids, span_bias, groups, halves):
    rows, width = drafts.shape
    heads = span_bias.shape[0]
    size = width // heads
    return pl.pallas_call(
        lambda *refs: attend_kernel(groups, halves, span_bias.shape[1], *refs),
        out_shape=jax.ShapeDtypeStruct((rows, width), jnp.bfloat16),
        grid_spec=pltpu.PrefetchScalarGridSpec(
            num_scalar_prefetch=1,
            grid=(heads,),
            in_specs=[
                pl.BlockSpec(memory_space=pltpu.SMEM),
                pl.BlockSpec((rows, size), lambda h, ids: (0, h)),
                pl.BlockSpec((R, size), lambda h, ids: (ids[0], h)),
                pl.BlockSpec((R, size), lambda h, ids: (ids[1], h)),
                pl.BlockSpec((1, 1, R), lambda h, ids: (ids[0], 0, 0)),
                pl.BlockSpec((1, 1, R), lambda h, ids: (ids[1], 0, 0)),
            ],
            out_specs=pl.BlockSpec((rows, size), lambda h, ids: (0, h)),
        ),
        cost_estimate=pl.CostEstimate(
            flops=8 * rows * R * width, bytes_accessed=8 * rows * width, transcendentals=2 * rows * R * heads
        ),
    )(ids, span_bias, drafts, keys, keys, spans, spans)

MESH = pl.DeviceIdType.MESH


def position():
    leaf, expert, half = (lax.axis_index(name) for name in ("leaf", "expert", "tensor"))
    across = expert + 1 - 2 * (expert % 2)
    along = (expert + 2) % 4
    return leaf, expert, half, across, along


def greet(partners):
    barrier = pltpu.get_barrier_semaphore()
    for partner in partners:
        pl.semaphore_signal(barrier, inc=1, device_id=partner, device_id_type=MESH)
    pl.semaphore_wait(barrier, len(partners))


def send(source, target, sems, index, device):
    copy = pltpu.make_async_remote_copy(
        src_ref=source,
        dst_ref=target,
        send_sem=sems.at[0, index],
        recv_sem=sems.at[1, index],
        device_id=device,
        device_id_type=MESH,
    )
    copy.start()
    return copy


def gather_kernel(
    leaves, rows, own_ref, merged_ref, gate_ref, up_ref, router_ref, hidden_ref, logit_ref, pair_ref,
    all_ref, gate_w, up_w, local, z_sem, x_sem, y_sem, a_sem, b_sem, swap_sem,
):
    leaf, expert, half, across, along = position()
    opposite = 3 - expert
    x_dev, y_dev = (leaf, across, half), (leaf, along, half)
    twin = (leaf, expert, 1 - half)
    z_devs = [((leaf + step) % leaves, expert, half) for step in range(1, leaves)]
    part = rows // 2

    def block(group, step, first=0, count=rows):
        return all_ref.at[(leaf + leaves - step) % leaves, half, group, pl.ds(first, count), :]

    keeps = [
        pltpu.make_async_copy(own_ref, block(expert, 0), local.at[0]),
        pltpu.make_async_copy(merged_ref, pair_ref.at[half], local.at[1]),
        pltpu.make_async_copy(gate_ref.at[0], gate_w, local.at[2]),
        pltpu.make_async_copy(up_ref.at[0], up_w, local.at[3]),
    ]
    keeps[0].start()
    greet([x_dev, y_dev, twin] + z_devs)
    z_copies = [None]
    for step in range(1, leaves):
        z_copies.append(send(own_ref, block(expert, 0), z_sem, step, z_devs[step - 1]))
    x_copies, y_copies, a_copies, b_copies, swaps = {}, {}, {}, {}, {}
    x_copies[0] = send(own_ref, block(expert, 0), x_sem, 0, x_dev)
    y_copies[0] = send(own_ref, block(expert, 0), y_sem, 0, y_dev)
    swaps[0] = [send(own_ref, block(expert, 0), swap_sem, 0, twin)]
    pair = send(merged_ref, pair_ref.at[half], swap_sem, 4 * leaves, twin)
    for keep in keeps[1:]:
        keep.start()
    order = [0] + sorted(range(1, leaves), key=lambda step: min(step, leaves - step))

    def exchange(group, step, kind):
        swaps[step].append(
            send(block(group, step), block(group, step), swap_sem, kind * leaves + step, twin)
        )

    def spread(step):
        z_copies[step].wait_recv()
        x_copies[step] = send(block(expert, step), block(expert, step), x_sem, step, x_dev)
        y_copies[step] = send(block(expert, step), block(expert, step), y_sem, step, y_dev)
        swaps[step] = []
        exchange(expert, step, 0)

    def forward(step):
        x_copies[step].wait_recv()
        a_copies[step] = send(
            block(across, step, 0, part), block(across, step, 0, part), a_sem, step, y_dev
        )
        y_copies[step].wait_recv()
        b_copies[step] = send(
            block(along, step, part, part), block(along, step, part, part), b_sem, step, x_dev
        )
        exchange(across, step, 1)
        exchange(along, step, 2)

    def corner(step):
        a_copies[step].wait_recv()
        b_copies[step].wait_recv()
        exchange(opposite, step, 3)

    def multiply(step):
        for copy in swaps[step]:
            copy.wait_recv()
        at = (leaf + leaves - step) % leaves
        width = all_ref.shape[-1]
        logit_ref[at] = jnp.dot(
            all_ref[at].reshape(-1, width), router_ref[...], preferred_element_type=jnp.float32
        )

        def tile(index, carry):
            columns = pl.ds(pl.multiple_of(index * 256, 256), 256)
            slab = all_ref[at].reshape(-1, width)
            gate_v = jnp.dot(slab, gate_w[:, columns], preferred_element_type=jnp.float32)
            up_v = jnp.dot(slab, up_w[:, columns], preferred_element_type=jnp.float32)
            hidden_ref[at, :, columns] = (gate_v / (1.0 + jnp.exp(-gate_v)) * up_v).astype(jnp.bfloat16)
            return carry

        lax.fori_loop(0, gate_w.shape[1] // 256, tile, 0)

    keeps[0].wait()
    for turn in range(1, leaves + 3):
        if turn < leaves:
            spread(order[turn])
        if turn <= leaves:
            forward(order[turn - 1])
        if 2 <= turn <= leaves + 1:
            corner(order[turn - 2])
        if turn == 2:
            for keep in keeps[1:]:
                keep.wait()
        if 3 <= turn:
            multiply(order[turn - 3])
    for step in order:
        for copy in swaps[step]:
            copy.wait_send()
        for group in (x_copies, y_copies, a_copies, b_copies):
            group[step].wait_send()
        if step > 0:
            z_copies[step].wait_send()
    pair.wait()


def gather_rows(normed, merged, w_gate, w_up, router, leaves, groups):
    rows, width = normed.shape
    units = w_gate.shape[2]
    slab = 2 * groups * rows
    dma = pltpu.SemaphoreType.DMA
    anywhere = pl.BlockSpec(memory_space=pl.ANY)
    inside = pl.BlockSpec(memory_space=pltpu.VMEM)
    return pl.pallas_call(
        lambda *refs: gather_kernel(leaves, rows, *refs),
        out_shape=(
            jax.ShapeDtypeStruct((leaves, slab, units), normed.dtype),
            jax.ShapeDtypeStruct((leaves, slab, router.shape[1]), jnp.float32),
            jax.ShapeDtypeStruct((2, rows, width), merged.dtype),
        ),
        in_specs=[anywhere] * 4 + [inside],
        out_specs=(inside, inside, anywhere),
        scratch_shapes=[
            pltpu.VMEM((leaves, 2, groups, rows, width), normed.dtype),
            pltpu.VMEM((width, units), w_gate.dtype),
            pltpu.VMEM((width, units), w_up.dtype),
            dma((4,)),
        ]
        + [dma((2, leaves))] * 5
        + [dma((2, 4 * leaves + 1))],
        compiler_params=pltpu.CompilerParams(
            collective_id=1, has_side_effects=True, vmem_limit_bytes=56 * 1024 * 1024
        ),
    )(normed, merged, w_gate, w_up, router)


def scatter_kernel(
    leaves, rows, hidden_ref, scale_ref, down_ref, out_ref, part_ref, twin_ref, down_w, in_a, in_b,
    mid_a, mid_b, last_a, last_b, sums, far, local, a_sem, b_sem, ma_sem, mb_sem, z_sem, swap_sem,
):
    leaf, expert, half, across, along = position()
    opposite = 3 - expert
    x_dev, y_dev = (leaf, across, half), (leaf, along, half)
    twin = (leaf, expert, 1 - half)
    z_devs = [((leaf + step) % leaves, expert, half) for step in range(1, leaves)]
    fetch = pltpu.make_async_copy(down_ref.at[0], down_w, local.at[0])
    fetch.start()
    greet([x_dev, y_dev, twin] + z_devs)
    fetch.wait()
    cut = rows // 2
    count = part_ref.shape[2]
    width = part_ref.shape[3]

    def block(group, step, first):
        start = group * rows + first
        return part_ref.at[step, half, pl.ds(pl.multiple_of(start, 16), cut), :]

    def wide(ref):
        return ref[...].astype(jnp.float32)

    order = list(range(1, leaves)) + [0]
    first, second, third, swaps = {}, {}, {}, {}

    def multiply(step):
        at = (leaf + step) % leaves

        def tile(index, carry):
            columns = pl.ds(pl.multiple_of(index * 512, 512), 512)
            product = jnp.dot(
                hidden_ref[at], down_w[:, columns], preferred_element_type=jnp.float32
            )
            product = (product * scale_ref[at][:, 0:1]).astype(jnp.bfloat16)
            part_ref[step, 0, :, columns] = product[:count]
            part_ref[step, 1, :, columns] = product[count:]
            return carry

        lax.fori_loop(0, width // 512, tile, 0)
        swaps[step] = send(part_ref.at[step, 1 - half], twin_ref.at[step], swap_sem, step, twin)

    def join(step):
        swaps[step].wait_recv()

        def piece(index, carry):
            at = pl.ds(pl.multiple_of(index * 16, 16), 16)
            part_ref[step, half, at, :] = (
                wide(part_ref.at[step, half, at, :]) + wide(twin_ref.at[step, at, :])
            ).astype(jnp.bfloat16)
            return carry

        lax.fori_loop(0, count // 16, piece, 0)
        first[step] = (
            send(block(opposite, step, 0), in_a.at[step, 1], a_sem, 2 * step + 1, x_dev),
            send(block(opposite, step, cut), in_b.at[step, 1], b_sem, 2 * step + 1, y_dev),
            send(block(across, step, 0), in_a.at[step, 0], a_sem, 2 * step, x_dev),
            send(block(along, step, cut), in_b.at[step, 0], b_sem, 2 * step, y_dev),
        )

    def middle(step):
        first[step][0].wait_recv()
        mid_a[step] = (wide(block(along, step, 0)) + wide(in_a.at[step, 1])).astype(jnp.bfloat16)
        to_y = send(mid_a.at[step], last_a.at[step], ma_sem, step, y_dev)
        first[step][1].wait_recv()
        mid_b[step] = (wide(block(across, step, cut)) + wide(in_b.at[step, 1])).astype(jnp.bfloat16)
        to_x = send(mid_b.at[step], last_b.at[step], mb_sem, step, x_dev)
        second[step] = (to_y, to_x)

    def finish(step):
        first[step][2].wait_recv()
        first[step][3].wait_recv()
        second[step][0].wait_recv()
        sum_a = wide(block(expert, step, 0)) + wide(in_a.at[step, 0]) + wide(last_a.at[step])
        sums[step, 0:cut, :] = sum_a.astype(jnp.bfloat16)
        second[step][1].wait_recv()
        sum_b = wide(block(expert, step, cut)) + wide(in_b.at[step, 0]) + wide(last_b.at[step])
        sums[step, cut:rows, :] = sum_b.astype(jnp.bfloat16)
        if step > 0:
            third[step] = send(sums.at[step], far.at[step], z_sem, step, z_devs[step - 1])

    for turn in range(leaves + 3):
        if turn < leaves:
            multiply(order[turn])
        if 1 <= turn <= leaves:
            join(order[turn - 1])
        if 2 <= turn <= leaves + 1:
            middle(order[turn - 2])
        if 3 <= turn:
            finish(order[turn - 3])
    total = wide(sums.at[0])
    for step in range(1, leaves):
        third[step].wait_recv()
        total = total + wide(far.at[step])
    out_ref[half] = total.astype(jnp.bfloat16)
    swapped = send(out_ref.at[half], out_ref.at[half], swap_sem, leaves, twin)
    for step in order:
        for copy in first[step] + second[step] + (swaps[step],):
            copy.wait_send()
        if step > 0:
            third[step].wait_send()
    swapped.wait()


def scatter_rows(hidden, scale, w_down, leaves, groups):
    rows, width = hidden.shape[1] // (2 * groups), w_down.shape[2]
    cut = rows // 2
    dma = pltpu.SemaphoreType.DMA
    kind = hidden.dtype
    inside = pl.BlockSpec(memory_space=pltpu.VMEM)
    return pl.pallas_call(
        lambda *refs: scatter_kernel(leaves, rows, *refs),
        out_shape=jax.ShapeDtypeStruct((2, rows, width), kind),
        in_specs=[inside, inside, pl.BlockSpec(memory_space=pl.ANY)],
        out_specs=inside,
        scratch_shapes=[
            pltpu.VMEM((leaves, 2, groups * rows, width), kind),
            pltpu.VMEM((leaves, groups * rows, width), kind),
            pltpu.VMEM(w_down.shape[1:], kind),
        ]
        + [pltpu.VMEM((leaves, 2, cut, width), kind)] * 2
        + [pltpu.VMEM((leaves, cut, width), kind)] * 4
        + [pltpu.VMEM((leaves, rows, width), kind)] * 2
        + [dma((1,))]
        + [dma((2, 2 * leaves))] * 2
        + [dma((2, leaves))] * 3
        + [dma((2, leaves + 1))],
        compiler_params=pltpu.CompilerParams(
            collective_id=2, has_side_effects=True, vmem_limit_bytes=56 * 1024 * 1024
        ),
    )(hidden, scale, w_down)


def per_device(
    drafts,
    children,
    child_order,
    spans,
    span_bias,
    out_weight,
    norm_gain,
    router,
    routes,
    w_gate,
    w_up,
    w_down,
):
    leaves = lax.axis_size("leaf")
    groups = lax.axis_size("expert")
    halves = lax.axis_size("tensor")
    width = out_weight.shape[1]
    rows = drafts.shape[0] // (groups * halves)
    parent = lax.axis_index("leaf")
    expert = lax.axis_index("expert")

    keys = lax.all_gather(children, "leaf", axis=0, tiled=True)
    key_spans = lax.all_gather(spans, "leaf", axis=0, tiled=True).reshape(-1, 1, R)
    all_routes = lax.all_gather(routes, ("leaf", "expert"), axis=0, tiled=True)
    draft_rows = lax.all_to_all(
        drafts, ("expert", "tensor"), split_axis=0, concat_axis=1, tiled=True
    )
    places = jnp.arange(child_order.shape[0], dtype=jnp.int32)
    ids = jnp.stack(
        [
            jnp.sum(jnp.where(child_order == 2 * parent, places, 0)),
            jnp.sum(jnp.where(child_order == 2 * parent + 1, places, 0)),
        ]
    ).astype(jnp.int32)
    ids, all_routes, draft_rows = lax.optimization_barrier((ids, all_routes, draft_rows))
    attended = attend(drafts, keys, key_spans, ids, span_bias, groups, halves)
    term = jnp.dot(attended, out_weight, preferred_element_type=jnp.float32).astype(jnp.bfloat16)
    term = lax.psum_scatter(term, "tensor", scatter_dimension=0, tiled=True)
    term = lax.psum_scatter(term, "expert", scatter_dimension=0, tiled=True)
    merged = draft_rows.astype(jnp.float32) + term.astype(jnp.float32)
    mean_square = jnp.mean(merged * merged, axis=-1, keepdims=True)
    normed = (merged * lax.rsqrt(mean_square + 1e-05) * norm_gain).astype(jnp.bfloat16)

    in_kernels = groups == 4 and halves == 2 and rows == 32
    if in_kernels:
        wide_router = jnp.pad(router, ((0, 0), (0, 128 - router.shape[1])))
        hidden, logits, merged_all = gather_rows(
            normed, merged, w_gate, w_up, wide_router, leaves, groups
        )
        logits = logits[:, :, : router.shape[1]]
    else:
        every = lax.all_gather(normed, "leaf", axis=0, tiled=True)
        every = lax.all_gather(every, "expert", axis=0, tiled=True)
        every = lax.all_gather(every, "tensor", axis=0, tiled=True)
        merged_all = lax.all_gather(merged, "tensor", axis=0, tiled=True)
        every = every.reshape(halves, groups, leaves, rows, width).transpose(2, 0, 1, 3, 4)
        every = every.reshape(leaves, -1, width)
        logits = jnp.dot(every, router, preferred_element_type=jnp.float32)
        gate_v = jnp.dot(every, w_gate[0], preferred_element_type=jnp.float32)
        up_v = jnp.dot(every, w_up[0], preferred_element_type=jnp.float32)
        hidden = (jax.nn.silu(gate_v) * up_v).astype(jnp.bfloat16)
    merged_all = merged_all.reshape(-1, width)

    named = all_routes.reshape(leaves, groups, halves, rows, 2).transpose(0, 2, 1, 3, 4)
    named = named.reshape(leaves, -1, 2)
    hot = named[..., None] == jnp.arange(router.shape[1], dtype=jnp.int32)
    chosen = jnp.sum(jnp.where(hot, logits[:, :, None, :], 0.0), axis=-1)
    gates = jax.nn.softmax(chosen, axis=-1)
    gate = jnp.sum(jnp.where(named == expert, gates, 0.0), axis=-1, keepdims=True)

    if in_kernels:
        scale = jnp.broadcast_to(gate, gate.shape[:2] + (128,))
        mixed = scatter_rows(hidden, scale, w_down, leaves, groups).reshape(-1, width)
    else:
        part = jnp.dot(hidden, w_down[0], preferred_element_type=jnp.float32) * gate
        part = part.astype(jnp.bfloat16).reshape(leaves, halves, groups, rows, width)
        part = part.transpose(1, 2, 0, 3, 4).reshape(-1, width)
        part = lax.psum_scatter(part, "tensor", scatter_dimension=0, tiled=True)
        part = lax.psum_scatter(part, "expert", scatter_dimension=0, tiled=True)
        part = lax.psum_scatter(part, "leaf", scatter_dimension=0, tiled=True)
        mixed = lax.all_gather(part, "tensor", axis=0, tiled=True)
    return merged_all + mixed.astype(jnp.float32)


def solution(mesh):
    in_specs = (
        P("leaf", ("expert", "tensor")),
        P("leaf", ("expert", "tensor")),
        P(),
        P("leaf"),
        P(("expert", "tensor"), None),
        P(("expert", "tensor"), None),
        P(),
        P(),
        P(("leaf", "expert"), None),
        P("expert", None, ("leaf", "tensor")),
        P("expert", None, ("leaf", "tensor")),
        P("expert", ("leaf", "tensor"), None),
    )
    out_specs = P(("leaf", "expert"), None)
    return jax.shard_map(
        per_device, mesh=mesh, in_specs=in_specs, out_specs=out_specs, check_vma=False
    )
```

```python
import math

import jax
import jax.numpy as jnp
from jax import lax
from jax.experimental import pallas as pl
from jax.experimental.pallas import tpu as pltpu
from jax.sharding import PartitionSpec as P

R = 256


def attend_kernel(groups, halves, span_count, ids, bias_ref, q_ref, ka_ref, kb_ref, sa_ref, sb_ref, o_ref):
    head = pl.program_id(0)
    scale = 1.0 / math.sqrt(q_ref.shape[1])
    queries = q_ref[...]
    contract = (((1,), (1,)), ((), ()))

    def score(k_ref, s_ref):
        spans = s_ref[0]
        bias = jnp.zeros(spans.shape, jnp.float32)
        for span in range(span_count):
            bias = jnp.where(spans == span, bias_ref[head, span], bias)
        dots = lax.dot_general(queries, k_ref[...], contract, preferred_element_type=jnp.float32)
        return dots * scale + bias

    score_a = score(ka_ref, sa_ref)
    score_b = score(kb_ref, sb_ref)
    top = jnp.maximum(
        jnp.max(score_a, axis=-1, keepdims=True), jnp.max(score_b, axis=-1, keepdims=True)
    )
    weight_a = jnp.exp(score_a - top)
    weight_b = jnp.exp(score_b - top)
    total = jnp.sum(weight_a, axis=-1, keepdims=True) + jnp.sum(weight_b, axis=-1, keepdims=True)
    values = jnp.dot(
        weight_a.astype(jnp.bfloat16), ka_ref[...], preferred_element_type=jnp.float32
    ) + jnp.dot(weight_b.astype(jnp.bfloat16), kb_ref[...], preferred_element_type=jnp.float32)
    attended = (values / total).astype(jnp.bfloat16)
    rows = attended.shape[0] // (groups * halves)
    for group in range(groups):
        for half in range(halves):
            source = (group * halves + half) * rows
            target = (half * groups + group) * rows
            o_ref[target : target + rows, :] = attended[source : source + rows, :]


def attend(drafts, keys, spans, ids, span_bias, groups, halves):
    rows, width = drafts.shape
    heads = span_bias.shape[0]
    size = width // heads
    return pl.pallas_call(
        lambda *refs: attend_kernel(groups, halves, span_bias.shape[1], *refs),
        out_shape=jax.ShapeDtypeStruct((rows, width), jnp.bfloat16),
        grid_spec=pltpu.PrefetchScalarGridSpec(
            num_scalar_prefetch=1,
            grid=(heads,),
            in_specs=[
                pl.BlockSpec(memory_space=pltpu.SMEM),
                pl.BlockSpec((rows, size), lambda h, ids: (0, h)),
                pl.BlockSpec((R, size), lambda h, ids: (ids[0], h)),
                pl.BlockSpec((R, size), lambda h, ids: (ids[1], h)),
                pl.BlockSpec((1, 1, R), lambda h, ids: (ids[0], 0, 0)),
                pl.BlockSpec((1, 1, R), lambda h, ids: (ids[1], 0, 0)),
            ],
            out_specs=pl.BlockSpec((rows, size), lambda h, ids: (0, h)),
        ),
        cost_estimate=pl.CostEstimate(
            flops=8 * rows * R * width, bytes_accessed=8 * rows * width, transcendentals=2 * rows * R * heads
        ),
    )(ids, span_bias, drafts, keys, keys, spans, spans)

MESH = pl.DeviceIdType.MESH


def position():
    leaf, expert, half = (lax.axis_index(name) for name in ("leaf", "expert", "tensor"))
    across = expert + 1 - 2 * (expert % 2)
    along = (expert + 2) % 4
    return leaf, expert, half, across, along


def greet(partners):
    barrier = pltpu.get_barrier_semaphore()
    for partner in partners:
        pl.semaphore_signal(barrier, inc=1, device_id=partner, device_id_type=MESH)
    pl.semaphore_wait(barrier, len(partners))


def send(source, target, sems, index, device):
    copy = pltpu.make_async_remote_copy(
        src_ref=source,
        dst_ref=target,
        send_sem=sems.at[0, index],
        recv_sem=sems.at[1, index],
        device_id=device,
        device_id_type=MESH,
    )
    copy.start()
    return copy


def project_kernel(
    rows, rows_ref, weight_ref, out_ref, part_ref, twin_ref, weight, in_a, in_b, mid_a, mid_b,
    last_a, last_b, local, a_sem, b_sem, ma_sem, mb_sem, swap_sem,
):
    leaf, expert, half, across, along = position()
    opposite = 3 - expert
    x_dev, y_dev = (leaf, across, half), (leaf, along, half)
    twin = (leaf, expert, 1 - half)
    fetch = pltpu.make_async_copy(weight_ref, weight, local.at[0])
    fetch.start()
    greet([x_dev, y_dev, twin])
    fetch.wait()
    cut = rows // 2
    steps, _, count, chunk = part_ref.shape

    def block(group, step, first):
        start = group * rows + first
        return part_ref.at[step, half, pl.ds(pl.multiple_of(start, 16), cut), :]

    def wide(ref):
        return ref[...].astype(jnp.float32)

    first, second, swaps = {}, {}, {}

    def multiply(step):
        def tile(index, carry):
            columns = pl.ds(pl.multiple_of(index * 512, 512), 512)
            source = pl.ds(pl.multiple_of(step * chunk + index * 512, 512), 512)
            product = jnp.dot(
                rows_ref[...], weight[:, source], preferred_element_type=jnp.float32
            ).astype(jnp.bfloat16)
            part_ref[step, 0, :, columns] = product[:count]
            part_ref[step, 1, :, columns] = product[count:]
            return carry

        lax.fori_loop(0, chunk // 512, tile, 0)
        swaps[step] = send(part_ref.at[step, 1 - half], twin_ref.at[step], swap_sem, step, twin)

    def join(step):
        swaps[step].wait_recv()

        def piece(index, carry):
            at = pl.ds(pl.multiple_of(index * 16, 16), 16)
            part_ref[step, half, at, :] = (
                wide(part_ref.at[step, half, at, :]) + wide(twin_ref.at[step, at, :])
            ).astype(jnp.bfloat16)
            return carry

        lax.fori_loop(0, count // 16, piece, 0)
        first[step] = (
            send(block(opposite, step, 0), in_a.at[step, 1], a_sem, 2 * step + 1, x_dev),
            send(block(opposite, step, cut), in_b.at[step, 1], b_sem, 2 * step + 1, y_dev),
            send(block(across, step, 0), in_a.at[step, 0], a_sem, 2 * step, x_dev),
            send(block(along, step, cut), in_b.at[step, 0], b_sem, 2 * step, y_dev),
        )

    def middle(step):
        first[step][0].wait_recv()
        mid_a[step] = (wide(block(along, step, 0)) + wide(in_a.at[step, 1])).astype(jnp.bfloat16)
        to_y = send(mid_a.at[step], last_a.at[step], ma_sem, step, y_dev)
        first[step][1].wait_recv()
        mid_b[step] = (wide(block(across, step, cut)) + wide(in_b.at[step, 1])).astype(jnp.bfloat16)
        to_x = send(mid_b.at[step], last_b.at[step], mb_sem, step, x_dev)
        second[step] = (to_y, to_x)

    def finish(step):
        first[step][2].wait_recv()
        first[step][3].wait_recv()
        second[step][0].wait_recv()
        columns = slice(step * chunk, (step + 1) * chunk)
        out_ref[0:cut, columns] = (
            wide(block(expert, step, 0)) + wide(in_a.at[step, 0]) + wide(last_a.at[step])
        )
        second[step][1].wait_recv()
        out_ref[cut:rows, columns] = (
            wide(block(expert, step, cut)) + wide(in_b.at[step, 0]) + wide(last_b.at[step])
        )

    for turn in range(steps + 3):
        if turn < steps:
            multiply(turn)
        if 1 <= turn <= steps:
            join(turn - 1)
        if 2 <= turn <= steps + 1:
            middle(turn - 2)
        if 3 <= turn:
            finish(turn - 3)
    for step in range(steps):
        for copy in first[step] + second[step] + (swaps[step],):
            copy.wait_send()


def project_rows(attended, out_weight, groups):
    rows, width = attended.shape[0] // (2 * groups), out_weight.shape[1]
    cut, steps = rows // 2, 4
    chunk = width // steps
    dma = pltpu.SemaphoreType.DMA
    kind = attended.dtype
    inside = pl.BlockSpec(memory_space=pltpu.VMEM)
    return pl.pallas_call(
        lambda *refs: project_kernel(rows, *refs),
        out_shape=jax.ShapeDtypeStruct((rows, width), jnp.float32),
        in_specs=[inside, pl.BlockSpec(memory_space=pl.ANY)],
        out_specs=inside,
        scratch_shapes=[
            pltpu.VMEM((steps, 2, groups * rows, chunk), kind),
            pltpu.VMEM((steps, groups * rows, chunk), kind),
            pltpu.VMEM(out_weight.shape, kind),
        ]
        + [pltpu.VMEM((steps, 2, cut, chunk), kind)] * 2
        + [pltpu.VMEM((steps, cut, chunk), kind)] * 4
        + [dma((1,))]
        + [dma((2, 2 * steps))] * 2
        + [dma((2, steps))] * 3,
        compiler_params=pltpu.CompilerParams(
            collective_id=3, has_side_effects=True, vmem_limit_bytes=40 * 1024 * 1024
        ),
    )(attended, out_weight)


def gather_kernel(
    leaves, rows, own_ref, merged_ref, gate_ref, up_ref, router_ref, hidden_ref, logit_ref, pair_ref,
    all_ref, gate_w, up_w, local, z_sem, x_sem, y_sem, a_sem, b_sem, swap_sem,
):
    leaf, expert, half, across, along = position()
    opposite = 3 - expert
    x_dev, y_dev = (leaf, across, half), (leaf, along, half)
    twin = (leaf, expert, 1 - half)
    z_devs = [((leaf + step) % leaves, expert, half) for step in range(1, leaves)]
    part = rows // 2

    def block(group, step, first=0, count=rows):
        return all_ref.at[(leaf + leaves - step) % leaves, half, group, pl.ds(first, count), :]

    keeps = [
        pltpu.make_async_copy(own_ref, block(expert, 0), local.at[0]),
        pltpu.make_async_copy(merged_ref, pair_ref.at[half], local.at[1]),
        pltpu.make_async_copy(gate_ref.at[0], gate_w, local.at[2]),
        pltpu.make_async_copy(up_ref.at[0], up_w, local.at[3]),
    ]
    keeps[0].start()
    greet([x_dev, y_dev, twin] + z_devs)
    z_copies = [None]
    for step in range(1, leaves):
        z_copies.append(send(own_ref, block(expert, 0), z_sem, step, z_devs[step - 1]))
    x_copies, y_copies, a_copies, b_copies, swaps = {}, {}, {}, {}, {}
    x_copies[0] = send(own_ref, block(expert, 0), x_sem, 0, x_dev)
    y_copies[0] = send(own_ref, block(expert, 0), y_sem, 0, y_dev)
    swaps[0] = [send(own_ref, block(expert, 0), swap_sem, 0, twin)]
    pair = send(merged_ref, pair_ref.at[half], swap_sem, 4 * leaves, twin)
    for keep in keeps[1:]:
        keep.start()
    order = [0] + sorted(range(1, leaves), key=lambda step: min(step, leaves - step))

    def exchange(group, step, kind):
        swaps[step].append(
            send(block(group, step), block(group, step), swap_sem, kind * leaves + step, twin)
        )

    def spread(step):
        z_copies[step].wait_recv()
        x_copies[step] = send(block(expert, step), block(expert, step), x_sem, step, x_dev)
        y_copies[step] = send(block(expert, step), block(expert, step), y_sem, step, y_dev)
        swaps[step] = []
        exchange(expert, step, 0)

    def forward(step):
        x_copies[step].wait_recv()
        a_copies[step] = send(
            block(across, step, 0, part), block(across, step, 0, part), a_sem, step, y_dev
        )
        y_copies[step].wait_recv()
        b_copies[step] = send(
            block(along, step, part, part), block(along, step, part, part), b_sem, step, x_dev
        )
        exchange(across, step, 1)
        exchange(along, step, 2)

    def corner(step):
        a_copies[step].wait_recv()
        b_copies[step].wait_recv()
        exchange(opposite, step, 3)

    def multiply(step):
        for copy in swaps[step]:
            copy.wait_recv()
        at = (leaf + leaves - step) % leaves
        width = all_ref.shape[-1]
        logit_ref[at] = jnp.dot(
            all_ref[at].reshape(-1, width), router_ref[...], preferred_element_type=jnp.float32
        )

        def tile(index, carry):
            columns = pl.ds(pl.multiple_of(index * 256, 256), 256)
            slab = all_ref[at].reshape(-1, width)
            gate_v = jnp.dot(slab, gate_w[:, columns], preferred_element_type=jnp.float32)
            up_v = jnp.dot(slab, up_w[:, columns], preferred_element_type=jnp.float32)
            hidden_ref[at, :, columns] = (gate_v / (1.0 + jnp.exp(-gate_v)) * up_v).astype(jnp.bfloat16)
            return carry

        lax.fori_loop(0, gate_w.shape[1] // 256, tile, 0)

    keeps[0].wait()
    for turn in range(1, leaves + 3):
        if turn < leaves:
            spread(order[turn])
        if turn <= leaves:
            forward(order[turn - 1])
        if 2 <= turn <= leaves + 1:
            corner(order[turn - 2])
        if turn == 2:
            for keep in keeps[1:]:
                keep.wait()
        if 3 <= turn:
            multiply(order[turn - 3])
    for step in order:
        for copy in swaps[step]:
            copy.wait_send()
        for group in (x_copies, y_copies, a_copies, b_copies):
            group[step].wait_send()
        if step > 0:
            z_copies[step].wait_send()
    pair.wait()


def gather_rows(normed, merged, w_gate, w_up, router, leaves, groups):
    rows, width = normed.shape
    units = w_gate.shape[2]
    slab = 2 * groups * rows
    dma = pltpu.SemaphoreType.DMA
    anywhere = pl.BlockSpec(memory_space=pl.ANY)
    inside = pl.BlockSpec(memory_space=pltpu.VMEM)
    return pl.pallas_call(
        lambda *refs: gather_kernel(leaves, rows, *refs),
        out_shape=(
            jax.ShapeDtypeStruct((leaves, slab, units), normed.dtype),
            jax.ShapeDtypeStruct((leaves, slab, router.shape[1]), jnp.float32),
            jax.ShapeDtypeStruct((2, rows, width), merged.dtype),
        ),
        in_specs=[anywhere] * 4 + [inside],
        out_specs=(inside, inside, anywhere),
        scratch_shapes=[
            pltpu.VMEM((leaves, 2, groups, rows, width), normed.dtype),
            pltpu.VMEM((width, units), w_gate.dtype),
            pltpu.VMEM((width, units), w_up.dtype),
            dma((4,)),
        ]
        + [dma((2, leaves))] * 5
        + [dma((2, 4 * leaves + 1))],
        compiler_params=pltpu.CompilerParams(
            collective_id=1, has_side_effects=True, vmem_limit_bytes=56 * 1024 * 1024
        ),
    )(normed, merged, w_gate, w_up, router)


def scatter_kernel(
    leaves, rows, hidden_ref, scale_ref, down_ref, out_ref, part_ref, twin_ref, down_w, in_a, in_b,
    mid_a, mid_b, last_a, last_b, sums, far, local, a_sem, b_sem, ma_sem, mb_sem, z_sem, swap_sem,
):
    leaf, expert, half, across, along = position()
    opposite = 3 - expert
    x_dev, y_dev = (leaf, across, half), (leaf, along, half)
    twin = (leaf, expert, 1 - half)
    z_devs = [((leaf + step) % leaves, expert, half) for step in range(1, leaves)]
    fetch = pltpu.make_async_copy(down_ref.at[0], down_w, local.at[0])
    fetch.start()
    greet([x_dev, y_dev, twin] + z_devs)
    fetch.wait()
    cut = rows // 2
    count = part_ref.shape[2]
    width = part_ref.shape[3]

    def block(group, step, first):
        start = group * rows + first
        return part_ref.at[step, half, pl.ds(pl.multiple_of(start, 16), cut), :]

    def wide(ref):
        return ref[...].astype(jnp.float32)

    order = list(range(1, leaves)) + [0]
    first, second, third, swaps = {}, {}, {}, {}

    def multiply(step):
        at = (leaf + step) % leaves

        def tile(index, carry):
            columns = pl.ds(pl.multiple_of(index * 512, 512), 512)
            product = jnp.dot(
                hidden_ref[at], down_w[:, columns], preferred_element_type=jnp.float32
            )
            product = (product * scale_ref[at][:, 0:1]).astype(jnp.bfloat16)
            part_ref[step, 0, :, columns] = product[:count]
            part_ref[step, 1, :, columns] = product[count:]
            return carry

        lax.fori_loop(0, width // 512, tile, 0)
        swaps[step] = send(part_ref.at[step, 1 - half], twin_ref.at[step], swap_sem, step, twin)

    def join(step):
        swaps[step].wait_recv()

        def piece(index, carry):
            at = pl.ds(pl.multiple_of(index * 16, 16), 16)
            part_ref[step, half, at, :] = (
                wide(part_ref.at[step, half, at, :]) + wide(twin_ref.at[step, at, :])
            ).astype(jnp.bfloat16)
            return carry

        lax.fori_loop(0, count // 16, piece, 0)
        first[step] = (
            send(block(opposite, step, 0), in_a.at[step, 1], a_sem, 2 * step + 1, x_dev),
            send(block(opposite, step, cut), in_b.at[step, 1], b_sem, 2 * step + 1, y_dev),
            send(block(across, step, 0), in_a.at[step, 0], a_sem, 2 * step, x_dev),
            send(block(along, step, cut), in_b.at[step, 0], b_sem, 2 * step, y_dev),
        )

    def middle(step):
        first[step][0].wait_recv()
        mid_a[step] = (wide(block(along, step, 0)) + wide(in_a.at[step, 1])).astype(jnp.bfloat16)
        to_y = send(mid_a.at[step], last_a.at[step], ma_sem, step, y_dev)
        first[step][1].wait_recv()
        mid_b[step] = (wide(block(across, step, cut)) + wide(in_b.at[step, 1])).astype(jnp.bfloat16)
        to_x = send(mid_b.at[step], last_b.at[step], mb_sem, step, x_dev)
        second[step] = (to_y, to_x)

    def finish(step):
        first[step][2].wait_recv()
        first[step][3].wait_recv()
        second[step][0].wait_recv()
        sum_a = wide(block(expert, step, 0)) + wide(in_a.at[step, 0]) + wide(last_a.at[step])
        sums[step, 0:cut, :] = sum_a.astype(jnp.bfloat16)
        second[step][1].wait_recv()
        sum_b = wide(block(expert, step, cut)) + wide(in_b.at[step, 0]) + wide(last_b.at[step])
        sums[step, cut:rows, :] = sum_b.astype(jnp.bfloat16)
        if step > 0:
            third[step] = send(sums.at[step], far.at[step], z_sem, step, z_devs[step - 1])

    for turn in range(leaves + 3):
        if turn < leaves:
            multiply(order[turn])
        if 1 <= turn <= leaves:
            join(order[turn - 1])
        if 2 <= turn <= leaves + 1:
            middle(order[turn - 2])
        if 3 <= turn:
            finish(order[turn - 3])
    total = wide(sums.at[0])
    for step in range(1, leaves):
        third[step].wait_recv()
        total = total + wide(far.at[step])
    out_ref[half] = total.astype(jnp.bfloat16)
    swapped = send(out_ref.at[half], out_ref.at[half], swap_sem, leaves, twin)
    for step in order:
        for copy in first[step] + second[step] + (swaps[step],):
            copy.wait_send()
        if step > 0:
            third[step].wait_send()
    swapped.wait()


def scatter_rows(hidden, scale, w_down, leaves, groups):
    rows, width = hidden.shape[1] // (2 * groups), w_down.shape[2]
    cut = rows // 2
    dma = pltpu.SemaphoreType.DMA
    kind = hidden.dtype
    inside = pl.BlockSpec(memory_space=pltpu.VMEM)
    return pl.pallas_call(
        lambda *refs: scatter_kernel(leaves, rows, *refs),
        out_shape=jax.ShapeDtypeStruct((2, rows, width), kind),
        in_specs=[inside, inside, pl.BlockSpec(memory_space=pl.ANY)],
        out_specs=inside,
        scratch_shapes=[
            pltpu.VMEM((leaves, 2, groups * rows, width), kind),
            pltpu.VMEM((leaves, groups * rows, width), kind),
            pltpu.VMEM(w_down.shape[1:], kind),
        ]
        + [pltpu.VMEM((leaves, 2, cut, width), kind)] * 2
        + [pltpu.VMEM((leaves, cut, width), kind)] * 4
        + [pltpu.VMEM((leaves, rows, width), kind)] * 2
        + [dma((1,))]
        + [dma((2, 2 * leaves))] * 2
        + [dma((2, leaves))] * 3
        + [dma((2, leaves + 1))],
        compiler_params=pltpu.CompilerParams(
            collective_id=2, has_side_effects=True, vmem_limit_bytes=56 * 1024 * 1024
        ),
    )(hidden, scale, w_down)


def per_device(
    drafts,
    children,
    child_order,
    spans,
    span_bias,
    out_weight,
    norm_gain,
    router,
    routes,
    w_gate,
    w_up,
    w_down,
):
    leaves = lax.axis_size("leaf")
    groups = lax.axis_size("expert")
    halves = lax.axis_size("tensor")
    width = out_weight.shape[1]
    rows = drafts.shape[0] // (groups * halves)
    parent = lax.axis_index("leaf")
    expert = lax.axis_index("expert")

    keys = lax.all_gather(children, "leaf", axis=0, tiled=True)
    key_spans = lax.all_gather(spans, "leaf", axis=0, tiled=True).reshape(-1, 1, R)
    all_routes = lax.all_gather(routes, ("leaf", "expert"), axis=0, tiled=True)
    draft_rows = lax.all_to_all(
        drafts, ("expert", "tensor"), split_axis=0, concat_axis=1, tiled=True
    )
    places = jnp.arange(child_order.shape[0], dtype=jnp.int32)
    ids = jnp.stack(
        [
            jnp.sum(jnp.where(child_order == 2 * parent, places, 0)),
            jnp.sum(jnp.where(child_order == 2 * parent + 1, places, 0)),
        ]
    ).astype(jnp.int32)
    ids, all_routes, draft_rows = lax.optimization_barrier((ids, all_routes, draft_rows))
    attended = attend(drafts, keys, key_spans, ids, span_bias, groups, halves)
    in_kernels = groups == 4 and halves == 2 and rows == 32
    if in_kernels:
        term = project_rows(attended, out_weight, groups)
    else:
        term = jnp.dot(attended, out_weight, preferred_element_type=jnp.float32)
        term = term.astype(jnp.bfloat16)
        term = lax.psum_scatter(term, "tensor", scatter_dimension=0, tiled=True)
        term = lax.psum_scatter(term, "expert", scatter_dimension=0, tiled=True)
    merged = draft_rows.astype(jnp.float32) + term.astype(jnp.float32)
    mean_square = jnp.mean(merged * merged, axis=-1, keepdims=True)
    normed = (merged * lax.rsqrt(mean_square + 1e-05) * norm_gain).astype(jnp.bfloat16)

    if in_kernels:
        wide_router = jnp.pad(router, ((0, 0), (0, 128 - router.shape[1])))
        hidden, logits, merged_all = gather_rows(
            normed, merged, w_gate, w_up, wide_router, leaves, groups
        )
        logits = logits[:, :, : router.shape[1]]
    else:
        every = lax.all_gather(normed, "leaf", axis=0, tiled=True)
        every = lax.all_gather(every, "expert", axis=0, tiled=True)
        every = lax.all_gather(every, "tensor", axis=0, tiled=True)
        merged_all = lax.all_gather(merged, "tensor", axis=0, tiled=True)
        every = every.reshape(halves, groups, leaves, rows, width).transpose(2, 0, 1, 3, 4)
        every = every.reshape(leaves, -1, width)
        logits = jnp.dot(every, router, preferred_element_type=jnp.float32)
        gate_v = jnp.dot(every, w_gate[0], preferred_element_type=jnp.float32)
        up_v = jnp.dot(every, w_up[0], preferred_element_type=jnp.float32)
        hidden = (jax.nn.silu(gate_v) * up_v).astype(jnp.bfloat16)
    merged_all = merged_all.reshape(-1, width)

    named = all_routes.reshape(leaves, groups, halves, rows, 2).transpose(0, 2, 1, 3, 4)
    named = named.reshape(leaves, -1, 2)
    hot = named[..., None] == jnp.arange(router.shape[1], dtype=jnp.int32)
    chosen = jnp.sum(jnp.where(hot, logits[:, :, None, :], 0.0), axis=-1)
    gates = jax.nn.softmax(chosen, axis=-1)
    gate = jnp.sum(jnp.where(named == expert, gates, 0.0), axis=-1, keepdims=True)

    if in_kernels:
        scale = jnp.broadcast_to(gate, gate.shape[:2] + (128,))
        mixed = scatter_rows(hidden, scale, w_down, leaves, groups).reshape(-1, width)
    else:
        part = jnp.dot(hidden, w_down[0], preferred_element_type=jnp.float32) * gate
        part = part.astype(jnp.bfloat16).reshape(leaves, halves, groups, rows, width)
        part = part.transpose(1, 2, 0, 3, 4).reshape(-1, width)
        part = lax.psum_scatter(part, "tensor", scatter_dimension=0, tiled=True)
        part = lax.psum_scatter(part, "expert", scatter_dimension=0, tiled=True)
        part = lax.psum_scatter(part, "leaf", scatter_dimension=0, tiled=True)
        mixed = lax.all_gather(part, "tensor", axis=0, tiled=True)
    return merged_all + mixed.astype(jnp.float32)


def solution(mesh):
    in_specs = (
        P("leaf", ("expert", "tensor")),
        P("leaf", ("expert", "tensor")),
        P(),
        P("leaf"),
        P(("expert", "tensor"), None),
        P(("expert", "tensor"), None),
        P(),
        P(),
        P(("leaf", "expert"), None),
        P("expert", None, ("leaf", "tensor")),
        P("expert", None, ("leaf", "tensor")),
        P("expert", ("leaf", "tensor"), None),
    )
    out_specs = P(("leaf", "expert"), None)
    return jax.shard_map(
        per_device, mesh=mesh, in_specs=in_specs, out_specs=out_specs, check_vma=False
    )
```
